512 devices in a mesh: surf: 16 (over x, y_lo, core), src: 32 (over z, y_hi).
Axes of the slice: x: 4, y: 4 (y_hi: 2, y_lo: 2; y = y_hi * 2 + y_lo), z: 16, core: 2. Of those that a mesh axis runs over, the one named last changes fastest.
Arguments:
- source_spectrum: bfloat16 [2, 2, 8192, 8192], P(None, None, 'src', 'surf'), may hold values from -6 to 6
- surf_freq: bfloat16 [2, 2, 8192, 2048], P(None, None, 'surf', 'src'), may hold values from -0.0625 to 0.0625
- centers: int32 [256], P('src'), may hold values from 0 to 8191
- counts: int32 [8192], P('surf'), may hold values from 1 to 2048
Outputs:
- multiples: float32 [2, 2, 8192, 2048], P(None, None, 'src', 'surf')
The draws below stay inside these ranges and needn't reach their ends.
All inputs are finite; a program needn't handle non-finite values.
Results may differ from the reference program's by a relative error of at most 0.00099.
Values may be sent and summed in bfloat16 or wider, within the bound.
No kernel may reach another device: no remote copies, remote signals or barrier semaphores. Data moves between devices by JAX's collectives and lax.ppermute only.
A program may use at most 64 MiB of HBM per device.

```python
import jax
import jax.numpy as jnp
from jax import lax

X = 8192
R = 2048
NF = 2
BLOCK = 32
S = 8192
APER = 2048
RAMP = 1024
N_SURF = 16


def touch_ends(result, own_key, least, largest):
    longest = result.shape.index(max(result.shape))
    spots = []
    for shift in (0, 1):
        where = [jax.random.randint(jax.random.fold_in(own_key, axis), (), 0, length) for axis, length in enumerate(result.shape)]
        where[longest] = (where[longest] + shift) % result.shape[longest]
        spots.append(tuple(where))
    return result.at[spots[0]].set(least).at[spots[1]].set(largest)


def shard_levels(key, shape, shards, least, largest):
    factor_of = 1.0
    for position, parts in shards:
        heights = jax.random.uniform(jax.random.fold_in(jax.random.fold_in(key, 6), position), (parts,), jnp.float32, least / len(shards), largest / len(shards))
        factor_of = factor_of * jnp.repeat(jnp.exp(heights), shape[position] // parts).reshape((-1,) + (1,) * (len(shape) - 1 - position))
    return factor_of


def bell_draw(own_key, dims, deviation, reach, cuts=(), kind=jnp.bfloat16):
    loudness = shard_levels(own_key, dims, cuts, -0.22, 0.18) if cuts else 1.0
    values = jax.random.normal(own_key, dims, jnp.float32) * deviation * loudness
    return jnp.minimum(jnp.maximum(values, -reach), reach).astype(kind)


def setup_inputs(seed: int = 0) -> dict:
    key_of = jax.random.split(jax.random.key(seed), 5)
    source_spectrum = bell_draw(key_of[0], (NF, 2, S, X), 1.0, 6.0, ((2, 32), (3, 16)))
    surf_freq = bell_draw(key_of[1], (NF, 2, X, R), X ** -0.5, 0.0625, ((2, 16), (3, 32)))
    centers = touch_ends(jax.random.randint(key_of[2], (S // BLOCK,), 0, X), jax.random.fold_in(key_of[2], 1), 0, X - 1).astype(jnp.int32)
    counts = touch_ends(jax.random.randint(key_of[3], (X,), 1, R + 1), jax.random.fold_in(key_of[3], 1), 1, R).astype(jnp.int32)
    return {"source_spectrum": source_spectrum, "surf_freq": surf_freq, "centers": centers, "counts": counts}


def complex_matrix_block(left_operand, right_operand):
    left_operand = left_operand.astype(jnp.float32)
    right_operand = right_operand.astype(jnp.float32)
    real_values = jnp.einsum("hbp,hpw->hbw", left_operand[:, 0], right_operand[:, 0], precision=lax.Precision.HIGHEST) - jnp.einsum("hbp,hpw->hbw", left_operand[:, 1], right_operand[:, 1], precision=lax.Precision.HIGHEST)
    imaginary_values = jnp.einsum("hbp,hpw->hbw", left_operand[:, 0], right_operand[:, 1], precision=lax.Precision.HIGHEST) + jnp.einsum("hbp,hpw->hbw", left_operand[:, 1], right_operand[:, 0], precision=lax.Precision.HIGHEST)
    return jnp.stack([real_values, imaginary_values], axis=1)


def reference(source_spectrum, surf_freq, centers, counts):
    center_rows = jnp.repeat(centers, BLOCK).astype(jnp.float32)
    positions = jnp.arange(X, dtype=jnp.int32).astype(jnp.float32)
    distance = jnp.abs(positions[None, :] - center_rows[:, None])
    taper = jnp.clip((APER + RAMP - distance) / RAMP, 0.0, 1.0).astype(jnp.float32)
    live = (jnp.arange(R, dtype=jnp.int32)[None, :] < counts[:, None]).astype(jnp.float32)
    left_operand = (source_spectrum.astype(jnp.float32) * taper[None, None]).astype(jnp.bfloat16)
    right_operand = (surf_freq.astype(jnp.float32) * live[None, None]).astype(jnp.bfloat16)
    width = X // N_SURF
    total = jnp.zeros((NF, 2, S, R), jnp.float32)
    for block in range(N_SURF):
        part = complex_matrix_block(left_operand[..., block * width:(block + 1) * width], right_operand[:, :, block * width:(block + 1) * width, :])
        total = total + part
    return total
```

```python
import itertools

import jax
import jax.numpy as jnp
from jax import lax
from jax.experimental import pallas as pl
from jax.experimental.pallas import tpu as pltpu
from jax.sharding import PartitionSpec as P

BLOCK = 32
APER = 2048
RAMP = 1024
AXES = ("surf", "src")
NX, NYL, NC, NZ, NH = 4, 2, 2, 16, 2
ROWS = 256
HALF = 512
LANES = 128
COLS = 64
MSG = 272
SHIFT = 31
VMEM_LIMIT = 48 * 1024 * 1024


def flat(x, yl, c, z, h):
    return ((x * NYL + yl) * NC + c) * NZ * NH + z * NH + h


COORDS = list(itertools.product(range(NX), range(NYL), range(NC), range(NZ), range(NH)))


def groups(key):
    found = {}
    for place in COORDS:
        found.setdefault(key(*place), []).append(flat(*place))
    return list(found.values())


CORE_PAIRS = [(flat(*p), flat(p[0], p[1], 1 - p[2], p[3], p[4])) for p in COORDS]
HALF_PAIRS = [(flat(*p), flat(p[0], p[1], p[2], p[3], 1 - p[4])) for p in COORDS]
ALONG_Z = groups(lambda x, yl, c, z, h: (x, yl, c, h))
PLANE_CHIPS = groups(lambda x, yl, c, z, h: (c, z, h))
CORE_HALF = groups(lambda x, yl, c, z, h: (x, yl, z))


def params():
    return pltpu.CompilerParams(vmem_limit_bytes=VMEM_LIMIT)


def prepare_kernel(where, centers, spectrum, surf, counts, keep_a, keep_b, sent):
    core = where[0]
    first = where[1] * HALF
    column0 = where[2] * COLS
    positions = (first + lax.broadcasted_iota(jnp.int32, (1, HALF), 1)).astype(jnp.float32)
    for f, to_send in ((core, False), (1 - core, True)):
        for part in range(2):
            for block in range(ROWS // BLOCK):
                rows = slice(block * BLOCK, (block + 1) * BLOCK)
                distance = jnp.abs(positions - centers[block].astype(jnp.float32))
                taper = jnp.clip((APER + RAMP - distance) / RAMP, 0.0, 1.0)
                values = (spectrum[f, part, rows, :].astype(jnp.float32) * taper).astype(jnp.bfloat16)
                if to_send:
                    for piece in range(HALF // LANES):
                        at = (part * (HALF // LANES) + piece) * ROWS + block * BLOCK
                        sent[at : at + BLOCK, :] = values[:, piece * LANES : (piece + 1) * LANES]
                else:
                    keep_a[part, rows, :] = values
    lane = lax.broadcasted_iota(jnp.int32, (1, LANES), 1)
    column = (column0 + jnp.where(lane < COLS, lane, lane - COLS)).astype(jnp.float32)
    base = 2 * (HALF // LANES) * ROWS
    for piece in range(HALF // LANES):
        rows = slice(piece * LANES, (piece + 1) * LANES)
        own = counts[piece : piece + 1, :].astype(jnp.float32)
        live = column < jnp.transpose(jnp.broadcast_to(own, (LANES, LANES)))
        for f, to_send in ((core, False), (1 - core, True)):
            both = jnp.concatenate(
                [surf[f, 0, rows, :].astype(jnp.float32), surf[f, 1, rows, :].astype(jnp.float32)], axis=1
            )
            both = jnp.where(live, both, 0.0)
            if to_send:
                sent[base + piece * LANES : base + (piece + 1) * LANES, :] = both.astype(jnp.bfloat16)
            else:
                keep_b[rows, :] = both.astype(jnp.bfloat16)


def prepare(where, centers, spectrum, surf, counts):
    vmem = pl.BlockSpec(memory_space=pltpu.VMEM)
    smem = pl.BlockSpec(memory_space=pltpu.SMEM)
    sent_rows = 2 * (HALF // LANES) * ROWS + HALF
    return pl.pallas_call(
        prepare_kernel,
        out_shape=[
            jax.ShapeDtypeStruct((2, ROWS, HALF), jnp.bfloat16),
            jax.ShapeDtypeStruct((HALF, LANES), jnp.bfloat16),
            jax.ShapeDtypeStruct((sent_rows, LANES), jnp.bfloat16),
        ],
        in_specs=[smem, smem, vmem, vmem, vmem],
        out_specs=[vmem, vmem, vmem],
        compiler_params=params(),
        cost_estimate=pl.CostEstimate(flops=4_000_000, bytes_accessed=3_000_000, transcendentals=0),
        name="prepare",
    )(where, centers, spectrum, surf, counts)


def encode(values):
    values = values.astype(jnp.float32)
    size = jnp.abs(values)
    exponent = jnp.floor(jnp.log2(jnp.maximum(size, 2.0**-126)) + 0.002)
    mantissa = jnp.round((size * 2.0**64) * jnp.exp2(-57.0 - exponent))
    down = jnp.clip(-4.0 - exponent, 0.0, 127.0)
    code = jnp.where(values < 0, -mantissa, mantissa) * 128.0 + down
    return jnp.where(size == 0, 0.0, code).astype(jnp.int32).astype(jnp.int16)


def pack_kernel(where, keep_a, keep_b, received, a, code):
    core = where[0]
    mine = pl.multiple_of(core * HALF, HALF)
    other = pl.multiple_of((1 - core) * HALF, HALF)
    a[:, :, pl.ds(mine, HALF)] = keep_a[...]
    for part in range(2):
        for piece in range(HALF // LANES):
            at = (part * (HALF // LANES) + piece) * ROWS
            column = pl.multiple_of(other + piece * LANES, LANES)
            a[part, :, pl.ds(column, LANES)] = received[at : at + ROWS, :]
    base = 2 * (HALF // LANES) * ROWS
    code[pl.ds(mine, HALF), :] = encode(keep_b[...])
    code[pl.ds(other, HALF), :] = encode(received[base : base + HALF, :])


def pack(where, keep_a, keep_b, received):
    vmem = pl.BlockSpec(memory_space=pltpu.VMEM)
    return pl.pallas_call(
        pack_kernel,
        out_shape=[
            jax.ShapeDtypeStruct((2, ROWS, 2 * HALF), jnp.bfloat16),
            jax.ShapeDtypeStruct((2 * HALF, LANES), jnp.int16),
        ],
        in_specs=[pl.BlockSpec(memory_space=pltpu.SMEM), vmem, vmem, vmem],
        out_specs=[vmem, vmem],
        compiler_params=params(),
        cost_estimate=pl.CostEstimate(flops=2_000_000, bytes_accessed=2_500_000, transcendentals=300_000),
        name="pack",
    )(where, keep_a, keep_b, received)


def exponent_of(largest):
    return jnp.floor(jnp.log2(jnp.maximum(largest, 2.0**-100)) + 0.002) + 1.0


def store_scaled(out, values, shift):
    exponent = exponent_of(jnp.max(jnp.abs(values), axis=0, keepdims=True))
    scaled = jnp.clip(jnp.round(values * jnp.exp2(15.0 - exponent)), -32767.0, 32767.0)
    out[:ROWS, :] = scaled.astype(jnp.int32).astype(jnp.int16)
    below = jnp.broadcast_to(exponent - shift, (MSG - ROWS, LANES))
    out[ROWS:, :] = below.astype(jnp.int32).astype(jnp.int16)


def load_scaled(message):
    exponent = message[ROWS:, :].astype(jnp.int32).astype(jnp.float32)[:1, :]
    return message[:ROWS, :].astype(jnp.int32).astype(jnp.float32) * jnp.exp2(exponent - 15.0)


def product_kernel(where, own, partner, gathered, out, a):
    @pl.when(pl.program_id(0) == 0)
    def _():
        half = where[3]
        a[:, pl.ds(pl.multiple_of(half * ROWS, ROWS), ROWS), :] = own[...]
        a[:, pl.ds(pl.multiple_of((1 - half) * ROWS, ROWS), ROWS), :] = partner[...]

    decoded = []
    for block in range(2):
        code = gathered[block].astype(jnp.int32)
        mantissa = lax.shift_right_arithmetic(code, 7).astype(jnp.float32)
        down = jnp.bitwise_and(code, 127).astype(jnp.float32)
        decoded.append((mantissa * jnp.exp2((SHIFT - 11.0) - down)).astype(jnp.bfloat16))
    b = jnp.concatenate(decoded, axis=1)
    straight = jnp.dot(a[0], b, preferred_element_type=jnp.float32)
    crossed = jnp.dot(a[1], b, preferred_element_type=jnp.float32)
    real = lax.broadcasted_iota(jnp.int32, (1, LANES), 1) < COLS
    for block in range(2):
        lanes = slice(block * LANES, (block + 1) * LANES)
        turned = pltpu.roll(crossed[:, lanes], COLS, 1)
        values = straight[:, lanes] + jnp.where(real, -turned, turned)
        for half in range(2):
            store_scaled(out.at[0, block, half], values[half * ROWS : (half + 1) * ROWS], SHIFT)


def product(where, own, partner, gathered):
    k = 2 * HALF
    return pl.pallas_call(
        product_kernel,
        grid=(8,),
        out_shape=jax.ShapeDtypeStruct((8, 2, 2, MSG, LANES), jnp.int16),
        in_specs=[
            pl.BlockSpec(memory_space=pltpu.SMEM),
            pl.BlockSpec((2, ROWS, k), lambda g: (0, 0, 0)),
            pl.BlockSpec((2, ROWS, k), lambda g: (0, 0, 0)),
            pl.BlockSpec((2, k, LANES), lambda g: (g, 0, 0)),
        ],
        out_specs=pl.BlockSpec((1, 2, 2, MSG, LANES), lambda g: (g, 0, 0, 0, 0)),
        scratch_shapes=[pltpu.VMEM((2, 2 * ROWS, k), jnp.bfloat16)],
        compiler_params=params(),
        cost_estimate=pl.CostEstimate(flops=4_300_000_000, bytes_accessed=9_000_000, transcendentals=2_000_000),
        name="product",
    )(where, own, partner, gathered)


def add_kernel(arrived, out):
    total = load_scaled(arrived.at[0, 0, 0])
    for source in range(1, 8):
        total = total + load_scaled(arrived.at[source, 0, 0])
    store_scaled(out.at[0], total, 0)


def add(arrived):
    return pl.pallas_call(
        add_kernel,
        grid=(4,),
        out_shape=jax.ShapeDtypeStruct((4, MSG, LANES), jnp.int16),
        in_specs=[pl.BlockSpec((8, 1, 1, MSG, LANES), lambda g: (0, g // 2, g % 2, 0, 0))],
        out_specs=pl.BlockSpec((1, MSG, LANES), lambda g: (g, 0, 0)),
        compiler_params=params(),
        cost_estimate=pl.CostEstimate(flops=4_000_000, bytes_accessed=3_000_000, transcendentals=0),
        name="add",
    )(arrived)


def finish_kernel(arrived, out):
    real = lax.broadcasted_iota(jnp.int32, (1, LANES), 1) < COLS
    for f in range(2):
        low = load_scaled(arrived.at[2 * f])
        high = load_scaled(arrived.at[2 * f + 1])
        out[f, 0] = jnp.where(real, low, pltpu.roll(high, COLS, 1))
        out[f, 1] = jnp.where(real, pltpu.roll(low, COLS, 1), high)


def finish(arrived):
    vmem = pl.BlockSpec(memory_space=pltpu.VMEM)
    return pl.pallas_call(
        finish_kernel,
        out_shape=jax.ShapeDtypeStruct((2, 2, ROWS, LANES), jnp.float32),
        in_specs=[vmem],
        out_specs=vmem,
        compiler_params=params(),
        cost_estimate=pl.CostEstimate(flops=1_000_000, bytes_accessed=1_000_000, transcendentals=0),
        name="finish",
    )(arrived)


def shards(source_spectrum, surf_freq, centers, counts):
    surf = lax.axis_index("surf")
    src = lax.axis_index("src")
    where = jnp.stack([surf % 2, surf, src, src % 2]).astype(jnp.int32)
    keep_a, keep_b, sent = prepare(where, centers, source_spectrum, surf_freq, counts.reshape(4, LANES))
    received = lax.ppermute(sent, AXES, CORE_PAIRS)
    own, code = pack(where, keep_a, keep_b, received)
    partner = lax.ppermute(own, AXES, HALF_PAIRS)
    gathered = lax.all_gather(code, AXES, axis_index_groups=ALONG_Z, axis=0)
    messages = product(where, own, partner, gathered)
    arrived = lax.all_to_all(messages, AXES, 0, 0, axis_index_groups=PLANE_CHIPS)
    sums = add(arrived)
    last = lax.all_to_all(sums, AXES, 0, 0, axis_index_groups=CORE_HALF)
    return finish(last)


def solution(mesh):
    in_specs = (P(None, None, "src", "surf"), P(None, None, "surf", "src"), P("src"), P("surf"))
    out_specs = P(None, None, "src", "surf")
    return jax.shard_map(shards, mesh=mesh, in_specs=in_specs, out_specs=out_specs, check_vma=False)
```

```python
import itertools

import jax
import jax.numpy as jnp
from jax import lax
from jax.experimental import pallas as pl
from jax.experimental.pallas import tpu as pltpu
from jax.sharding import PartitionSpec as P

BLOCK = 32
APER = 2048
RAMP = 1024
AXES = ("surf", "src")
NX, NYL, NC, NZ, NH = 4, 2, 2, 16, 2
ROWS = 256
HALF = 512
LANES = 128
COLS = 64
MSG = 272
SHIFT = 31
VMEM_LIMIT = 24 * 1024 * 1024
ALL_VMEM = 62 * 1024 * 1024 + 512 * 1024


def flat(x, yl, c, z, h):
    return ((x * NYL + yl) * NC + c) * NZ * NH + z * NH + h


COORDS = list(itertools.product(range(NX), range(NYL), range(NC), range(NZ), range(NH)))


def groups(key):
    found = {}
    for place in COORDS:
        found.setdefault(key(*place), []).append(flat(*place))
    return list(found.values())


CORE_PAIRS = [(flat(*p), flat(p[0], p[1], 1 - p[2], p[3], p[4])) for p in COORDS]
HALF_PAIRS = [(flat(*p), flat(p[0], p[1], p[2], p[3], 1 - p[4])) for p in COORDS]
ALONG_Z = groups(lambda x, yl, c, z, h: (x, yl, c, h))
PLANE_CHIPS = groups(lambda x, yl, c, z, h: (c, z))


def params(limit=VMEM_LIMIT):
    return pltpu.CompilerParams(vmem_limit_bytes=limit)


def vmem():
    return pl.BlockSpec(memory_space=pltpu.VMEM)


def anywhere():
    return pl.BlockSpec(memory_space=pl.ANY)


def core_index():
    return lax.rem(lax.axis_index("surf"), NC)


def half_index():
    return lax.rem(lax.axis_index("src"), NH)


def prepare_kernel(spectrum_in, surf_in, counts_in, centers_in, keep_a, keep_b, sent, spectrum, surf, counts, centers, sems):
    core = core_index()
    copies = [
        pltpu.make_async_copy(centers_in, centers, sems.at[0]),
        pltpu.make_async_copy(counts_in, counts, sems.at[1]),
        pltpu.make_async_copy(surf_in, surf, sems.at[2]),
        pltpu.make_async_copy(spectrum_in, spectrum, sems.at[3]),
    ]
    for copy in copies:
        copy.start()
    for copy in copies[:3]:
        copy.wait()
    column = lax.axis_index("src") * COLS + lax.broadcasted_iota(jnp.int32, (COLS, LANES), 0)
    for piece in range(HALF // LANES):
        lanes = slice(piece * LANES, (piece + 1) * LANES)
        live = column < counts[piece : piece + 1, :]
        for f, to_send in ((core, False), (1 - core, True)):
            for part in range(2):
                values = jnp.where(live, surf[f, part, :, lanes].astype(jnp.float32), 0.0).astype(jnp.bfloat16)
                if to_send:
                    sent[2 * ROWS + part * COLS : 2 * ROWS + (part + 1) * COLS, lanes] = values
                else:
                    keep_b[part * COLS : (part + 1) * COLS, lanes] = values
    copies[3].wait()
    first = lax.axis_index("surf") * HALF
    positions = (first + lax.broadcasted_iota(jnp.int32, (1, HALF), 1)).astype(jnp.float32)
    for block in range(ROWS // BLOCK):
        rows = slice(block * BLOCK, (block + 1) * BLOCK)
        distance = jnp.abs(positions - centers[block].astype(jnp.float32))
        taper = jnp.clip((APER + RAMP - distance) / RAMP, 0.0, 1.0)
        for part in range(2):
            keep_a[part, rows, :] = (spectrum[core, part, rows, :].astype(jnp.float32) * taper).astype(jnp.bfloat16)
            values = (spectrum[1 - core, part, rows, :].astype(jnp.float32) * taper).astype(jnp.bfloat16)
            sent[part * ROWS + block * BLOCK : part * ROWS + (block + 1) * BLOCK, :] = values


def prepare(spectrum, surf, counts, centers):
    return pl.pallas_call(
        prepare_kernel,
        out_shape=[
            jax.ShapeDtypeStruct((2, ROWS, HALF), jnp.bfloat16),
            jax.ShapeDtypeStruct((2 * COLS, HALF), jnp.bfloat16),
            jax.ShapeDtypeStruct((2 * ROWS + 2 * COLS, HALF), jnp.bfloat16),
        ],
        in_specs=[anywhere()] * 4,
        out_specs=[vmem(), vmem(), vmem()],
        scratch_shapes=[
            pltpu.VMEM((2, 2, ROWS, HALF), jnp.bfloat16),
            pltpu.VMEM((2, 2, COLS, HALF), jnp.bfloat16),
            pltpu.VMEM((HALF // LANES, LANES), jnp.int32),
            pltpu.SMEM((ROWS // BLOCK,), jnp.int32),
            pltpu.SemaphoreType.DMA((4,)),
        ],
        compiler_params=params(ALL_VMEM),
        cost_estimate=pl.CostEstimate(flops=4_000_000, bytes_accessed=3_000_000, transcendentals=0),
        name="prepare",
    )(spectrum, surf, counts, centers)


def encode(values):
    values = values.astype(jnp.float32)
    size = jnp.abs(values)
    exponent = jnp.floor(jnp.log2(jnp.maximum(size, 2.0**-126)) + 0.002)
    mantissa = jnp.round((size * 2.0**64) * jnp.exp2(-57.0 - exponent))
    down = jnp.clip(-4.0 - exponent, 0.0, 127.0)
    code = jnp.where(values < 0, -mantissa, mantissa) * 128.0 + down
    return jnp.where(size == 0, 0.0, code).astype(jnp.int32).astype(jnp.int16)


def pack_kernel(keep_a, keep_b, received, a, code):
    core = core_index()
    mine = pl.multiple_of(core * HALF, HALF)
    other = pl.multiple_of((1 - core) * HALF, HALF)
    code[:, pl.ds(mine, HALF)] = encode(keep_b[...])
    code[:, pl.ds(other, HALF)] = encode(received[2 * ROWS :, :])
    for part in range(2):
        a[:, pl.ds(pl.multiple_of(part * 2 * HALF + mine, HALF), HALF)] = keep_a[part]
        a[:, pl.ds(pl.multiple_of(part * 2 * HALF + other, HALF), HALF)] = received[part * ROWS : (part + 1) * ROWS, :]


def pack(keep_a, keep_b, received):
    return pl.pallas_call(
        pack_kernel,
        out_shape=[
            jax.ShapeDtypeStruct((ROWS, 4 * HALF), jnp.bfloat16),
            jax.ShapeDtypeStruct((2 * COLS, 2 * HALF), jnp.int16),
        ],
        in_specs=[vmem()] * 3,
        out_specs=[vmem()] * 2,
        compiler_params=params(),
        cost_estimate=pl.CostEstimate(flops=2_000_000, bytes_accessed=2_500_000, transcendentals=300_000),
        name="pack",
    )(keep_a, keep_b, received)


def exponent_of(largest):
    return jnp.floor(jnp.log2(jnp.maximum(largest, 2.0**-100)) + 0.002) + 1.0


def store_scaled(out, values, shift):
    exponent = exponent_of(jnp.max(jnp.abs(values), axis=0, keepdims=True))
    scaled = jnp.clip(jnp.round(values * jnp.exp2(15.0 - exponent)), -32767.0, 32767.0)
    out[:ROWS, :] = scaled.astype(jnp.int32).astype(jnp.int16)
    below = jnp.broadcast_to(exponent - shift, (MSG - ROWS, LANES))
    out[ROWS:, :] = below.astype(jnp.int32).astype(jnp.int16)


def load_scaled(message):
    exponent = message[ROWS:, :].astype(jnp.int32).astype(jnp.float32)[:1, :]
    return message[:ROWS, :].astype(jnp.int32).astype(jnp.float32) * jnp.exp2(exponent - 15.0)


def decode_pair(gathered, pair, b):
    k = 2 * HALF
    for block in range(2):
        for part in range(2):
            code = gathered[2 * pair + block, part * COLS : (part + 1) * COLS, :].astype(jnp.int32)
            mantissa = lax.shift_right_arithmetic(code, 7).astype(jnp.float32)
            down = jnp.bitwise_and(code, 127).astype(jnp.float32)
            piece = (mantissa * jnp.exp2((SHIFT - 11.0) - down)).astype(jnp.bfloat16)
            straight = block * LANES + part * COLS
            crossed = block * LANES + (1 - part) * COLS
            b[straight : straight + COLS, :k] = piece
            b[crossed : crossed + COLS, k:] = piece if part == 0 else -piece


def product_kernel(own, partner, gathered, out, a, b_even, b_odd):
    half = half_index()
    a[pl.ds(pl.multiple_of(half * ROWS, ROWS), ROWS), :] = own[...]
    a[pl.ds(pl.multiple_of((1 - half) * ROWS, ROWS), ROWS), :] = partner[...]
    pairs = NZ // 2
    decode_pair(gathered, 0, b_even)
    for pair in range(pairs):
        now, later = (b_even, b_odd) if pair % 2 == 0 else (b_odd, b_even)
        if pair + 1 < pairs:
            decode_pair(gathered, pair + 1, later)
        values = lax.dot_general(a[...], now[...], (((1,), (1,)), ((), ())), preferred_element_type=jnp.float32)
        for half in range(2):
            for core in range(2):
                tile = values[half * ROWS : (half + 1) * ROWS, core * LANES : (core + 1) * LANES]
                store_scaled(out.at[2 * pair + half, core], tile, SHIFT)


def product(own, partner, gathered):
    k = 2 * HALF
    return pl.pallas_call(
        product_kernel,
        out_shape=jax.ShapeDtypeStruct((16, 2, MSG, LANES), jnp.int16),
        in_specs=[vmem()] * 3,
        out_specs=vmem(),
        scratch_shapes=[
            pltpu.VMEM((2 * ROWS, 2 * k), jnp.bfloat16),
            pltpu.VMEM((2 * LANES, 2 * k), jnp.bfloat16),
            pltpu.VMEM((2 * LANES, 2 * k), jnp.bfloat16),
        ],
        compiler_params=params(),
        cost_estimate=pl.CostEstimate(flops=4_300_000_000, bytes_accessed=9_000_000, transcendentals=2_000_000),
        name="product",
    )(own, partner, gathered)


def add_kernel(arrived, keep, sent):
    core = core_index()
    for out, which in ((keep, core), (sent, 1 - core)):
        for half in range(2):
            total = load_scaled(arrived.at[half, which])
            for chip in range(1, 8):
                total = total + load_scaled(arrived.at[2 * chip + half, which])
            out[half] = total


def add(arrived):
    return pl.pallas_call(
        add_kernel,
        out_shape=[jax.ShapeDtypeStruct((2, ROWS, LANES), jnp.float32)] * 2,
        in_specs=[vmem()],
        out_specs=[vmem()] * 2,
        compiler_params=params(),
        cost_estimate=pl.CostEstimate(flops=4_000_000, bytes_accessed=3_000_000, transcendentals=0),
        name="add",
    )(arrived)


def finish_kernel(keep, received, out):
    core = core_index()
    low = lax.broadcasted_iota(jnp.int32, (1, LANES), 1) < COLS
    for values, f in ((keep, core), (received, 1 - core)):
        out[f, 0] = jnp.where(low, values[0], pltpu.roll(values[1], COLS, 1))
        out[f, 1] = jnp.where(low, pltpu.roll(values[0], COLS, 1), values[1])


def finish(keep, received):
    return pl.pallas_call(
        finish_kernel,
        out_shape=jax.ShapeDtypeStruct((2, 2, ROWS, LANES), jnp.float32),
        in_specs=[vmem()] * 2,
        out_specs=vmem(),
        compiler_params=params(),
        cost_estimate=pl.CostEstimate(flops=1_000_000, bytes_accessed=1_000_000, transcendentals=0),
        name="finish",
    )(keep, received)


def shards(source_spectrum, surf_freq, centers, counts):
    surf_t = jnp.swapaxes(surf_freq, 2, 3)
    keep_a, keep_b, sent = prepare(source_spectrum, surf_t, counts.reshape(HALF // LANES, LANES), centers)
    received = lax.ppermute(sent, AXES, CORE_PAIRS)
    own, code = pack(keep_a, keep_b, received)
    partner = lax.ppermute(own, AXES, HALF_PAIRS)
    gathered = lax.all_gather(code, AXES, axis_index_groups=ALONG_Z, axis=0)
    arrived = lax.all_to_all(product(own, partner, gathered), AXES, 0, 0, axis_index_groups=PLANE_CHIPS)
    keep, sent = add(arrived)
    return finish(keep, lax.ppermute(sent, AXES, CORE_PAIRS))


def solution(mesh):
    in_specs = (P(None, None, "src", "surf"), P(None, None, "surf", "src"), P("src"), P("surf"))
    out_specs = P(None, None, "src", "surf")
    return jax.shard_map(shards, mesh=mesh, in_specs=in_specs, out_specs=out_specs, check_vma=False)
```

```python
import functools
import itertools

import jax
import jax.numpy as jnp
from jax import lax
from jax.experimental import pallas as pl
from jax.experimental.pallas import tpu as pltpu
from jax.sharding import PartitionSpec as P

BLOCK = 32
APER = 2048
RAMP = 1024
AXES = ("surf", "src")
NX, NYL, NC, NZ, NH = 4, 2, 2, 16, 2
ROWS = 256
HALF = 512
LANES = 128
COLS = 64
MSG = 528
SHIFT = 31
VMEM_LIMIT = 24 * 1024 * 1024
ALL_VMEM = 62 * 1024 * 1024 + 512 * 1024


def flat(x, yl, c, z, h):
    return ((x * NYL + yl) * NC + c) * NZ * NH + z * NH + h


COORDS = list(itertools.product(range(NX), range(NYL), range(NC), range(NZ), range(NH)))


def groups(key):
    found = {}
    for place in COORDS:
        found.setdefault(key(*place), []).append(flat(*place))
    return list(found.values())


CORE_PAIRS = [(flat(*p), flat(p[0], p[1], 1 - p[2], p[3], p[4])) for p in COORDS]
HALF_PAIRS = [(flat(*p), flat(p[0], p[1], p[2], p[3], 1 - p[4])) for p in COORDS]
ALONG_Z = groups(lambda x, yl, c, z, h: (x, yl, c, h))
PLANE_CHIPS = groups(lambda x, yl, c, z, h: (c, z))


def params(limit=VMEM_LIMIT):
    return pltpu.CompilerParams(vmem_limit_bytes=limit)


def vmem():
    return pl.BlockSpec(memory_space=pltpu.VMEM)


def anywhere():
    return pl.BlockSpec(memory_space=pl.ANY)


def core_index():
    return lax.rem(lax.axis_index("surf"), NC)


def half_index():
    return lax.rem(lax.axis_index("src"), NH)


def prepare_kernel(to_send, spectrum_in, surf_in, counts_in, centers_in, out, spectrum, surf, counts, centers, sems):
    f = 1 - core_index() if to_send else core_index()
    copies = [
        pltpu.make_async_copy(counts_in, counts, sems.at[0]),
        pltpu.make_async_copy(centers_in, centers, sems.at[1]),
        pltpu.make_async_copy(surf_in.at[f], surf, sems.at[2]),
        pltpu.make_async_copy(spectrum_in.at[f], spectrum, sems.at[3]),
    ]
    for copy in copies:
        copy.start()
    for copy in copies[:3]:
        copy.wait()
    column = lax.axis_index("src") * COLS + lax.broadcasted_iota(jnp.int32, (COLS, LANES), 0)
    for piece in range(HALF // LANES):
        lanes = slice(piece * LANES, (piece + 1) * LANES)
        live = column < counts[piece : piece + 1, :]
        for part in range(2):
            values = jnp.where(live, surf[part, :, lanes].astype(jnp.float32), 0.0).astype(jnp.bfloat16)
            out[2 * ROWS + part * COLS : 2 * ROWS + (part + 1) * COLS, lanes] = values
    copies[3].wait()
    first = lax.axis_index("surf") * HALF
    positions = (first + lax.broadcasted_iota(jnp.int32, (1, HALF), 1)).astype(jnp.float32)
    for block in range(ROWS // BLOCK):
        rows = slice(block * BLOCK, (block + 1) * BLOCK)
        distance = jnp.abs(positions - centers[block].astype(jnp.float32))
        taper = jnp.clip((APER + RAMP - distance) / RAMP, 0.0, 1.0)
        for part in range(2):
            values = (spectrum[part, rows, :].astype(jnp.float32) * taper).astype(jnp.bfloat16)
            out[part * ROWS + block * BLOCK : part * ROWS + (block + 1) * BLOCK, :] = values


def prepare(to_send, spectrum, surf, counts, centers):
    return pl.pallas_call(
        functools.partial(prepare_kernel, to_send),
        out_shape=jax.ShapeDtypeStruct((2 * ROWS + 2 * COLS, HALF), jnp.bfloat16),
        in_specs=[anywhere()] * 4,
        out_specs=vmem(),
        scratch_shapes=[
            pltpu.VMEM((2, ROWS, HALF), jnp.bfloat16),
            pltpu.VMEM((2, COLS, HALF), jnp.bfloat16),
            pltpu.VMEM((HALF // LANES, LANES), jnp.int32),
            pltpu.SMEM((ROWS // BLOCK,), jnp.int32),
            pltpu.SemaphoreType.DMA((4,)),
        ],
        compiler_params=params(ALL_VMEM if to_send else VMEM_LIMIT),
        cost_estimate=pl.CostEstimate(flops=2_000_000, bytes_accessed=3_000_000, transcendentals=0),
        name="prepare_sent" if to_send else "prepare_kept",
    )(spectrum, surf, counts, centers)


def encode(values):
    values = values.astype(jnp.float32)
    size = jnp.abs(values)
    exponent = jnp.floor(jnp.log2(jnp.maximum(size, 2.0**-126)) + 0.002)
    mantissa = jnp.round((size * 2.0**64) * jnp.exp2(-57.0 - exponent))
    down = jnp.clip(-4.0 - exponent, 0.0, 127.0)
    code = jnp.where(values < 0, -mantissa, mantissa) * 128.0 + down
    return jnp.where(size == 0, 0.0, code).astype(jnp.int32).astype(jnp.int16)


def pack_kernel(kept, received, a, code):
    core = core_index()
    for values, which in ((kept, core), (received, 1 - core)):
        place = pl.multiple_of(which * HALF, HALF)
        code[:, pl.ds(place, HALF)] = encode(values[2 * ROWS :, :])
        for part in range(2):
            columns = pl.ds(pl.multiple_of(part * 2 * HALF + place, HALF), HALF)
            a[:, columns] = values[part * ROWS : (part + 1) * ROWS, :]


def pack(kept, received):
    return pl.pallas_call(
        pack_kernel,
        out_shape=[
            jax.ShapeDtypeStruct((ROWS, 4 * HALF), jnp.bfloat16),
            jax.ShapeDtypeStruct((2 * COLS, 2 * HALF), jnp.int16),
        ],
        in_specs=[vmem()] * 2,
        out_specs=[vmem()] * 2,
        compiler_params=params(),
        cost_estimate=pl.CostEstimate(flops=2_000_000, bytes_accessed=2_500_000, transcendentals=300_000),
        name="pack",
    )(kept, received)


def exponent_of(largest):
    return jnp.floor(jnp.log2(jnp.maximum(largest, 2.0**-100)) + 0.002) + 1.0


def store_scaled(out, tiles, shift):
    exponents = []
    for which, values in enumerate(tiles):
        exponent = exponent_of(jnp.max(jnp.abs(values), axis=0, keepdims=True))
        scaled = jnp.clip(jnp.round(values * jnp.exp2(15.0 - exponent)), -32767.0, 32767.0)
        out[which * ROWS : (which + 1) * ROWS, :] = scaled.astype(jnp.int32).astype(jnp.int16)
        exponents.append(exponent - shift)
    row = lax.broadcasted_iota(jnp.int32, (MSG - 2 * ROWS, LANES), 0)
    out[2 * ROWS :, :] = jnp.where(row == 0, exponents[0], exponents[1]).astype(jnp.int32).astype(jnp.int16)


def load_scaled(message, which):
    below = message[2 * ROWS :, :].astype(jnp.int32).astype(jnp.float32)
    exponent = jnp.where(which == 0, below[0:1, :], below[1:2, :])
    values = message[pl.ds(pl.multiple_of(which * ROWS, ROWS), ROWS), :]
    return values.astype(jnp.int32).astype(jnp.float32) * jnp.exp2(exponent - 15.0)


def decode_pair(gathered, pair, b):
    k = 2 * HALF
    for block in range(2):
        for part in range(2):
            code = gathered[2 * pair + block, part * COLS : (part + 1) * COLS, :].astype(jnp.int32)
            mantissa = lax.shift_right_arithmetic(code, 7).astype(jnp.float32)
            down = jnp.bitwise_and(code, 127).astype(jnp.float32)
            piece = (mantissa * jnp.exp2((SHIFT - 11.0) - down)).astype(jnp.bfloat16)
            straight = block * LANES + part * COLS
            crossed = block * LANES + (1 - part) * COLS
            b[straight : straight + COLS, :k] = piece
            b[crossed : crossed + COLS, k:] = piece if part == 0 else -piece


def product_kernel(own, partner, gathered, out, a, b_even, b_odd):
    half = half_index()
    a[pl.ds(pl.multiple_of(half * ROWS, ROWS), ROWS), :] = own[...]
    a[pl.ds(pl.multiple_of((1 - half) * ROWS, ROWS), ROWS), :] = partner[...]
    pairs = NZ // 2
    decode_pair(gathered, 0, b_even)
    for pair in range(pairs):
        now, later = (b_even, b_odd) if pair % 2 == 0 else (b_odd, b_even)
        if pair + 1 < pairs:
            decode_pair(gathered, pair + 1, later)
        values = lax.dot_general(a[...], now[...], (((1,), (1,)), ((), ())), preferred_element_type=jnp.float32)
        for half in range(2):
            rows = slice(half * ROWS, (half + 1) * ROWS)
            store_scaled(out.at[2 * pair + half], (values[rows, :LANES], values[rows, LANES:]), SHIFT)


def product(own, partner, gathered):
    k = 2 * HALF
    return pl.pallas_call(
        product_kernel,
        out_shape=jax.ShapeDtypeStruct((16, MSG, LANES), jnp.int16),
        in_specs=[vmem()] * 3,
        out_specs=vmem(),
        scratch_shapes=[
            pltpu.VMEM((2 * ROWS, 2 * k), jnp.bfloat16),
            pltpu.VMEM((2 * LANES, 2 * k), jnp.bfloat16),
            pltpu.VMEM((2 * LANES, 2 * k), jnp.bfloat16),
        ],
        compiler_params=params(),
        cost_estimate=pl.CostEstimate(flops=4_300_000_000, bytes_accessed=9_000_000, transcendentals=2_000_000),
        name="product",
    )(own, partner, gathered)


def add_kernel(arrived, keep, sent):
    core = core_index()
    for out, which in ((keep, core), (sent, 1 - core)):
        for half in range(2):
            total = load_scaled(arrived.at[half], which)
            for chip in range(1, 8):
                total = total + load_scaled(arrived.at[2 * chip + half], which)
            out[half] = total


def add(arrived):
    return pl.pallas_call(
        add_kernel,
        out_shape=[jax.ShapeDtypeStruct((2, ROWS, LANES), jnp.float32)] * 2,
        in_specs=[vmem()],
        out_specs=[vmem()] * 2,
        compiler_params=params(),
        cost_estimate=pl.CostEstimate(flops=4_000_000, bytes_accessed=3_000_000, transcendentals=0),
        name="add",
    )(arrived)


def finish_kernel(keep, received, out):
    core = core_index()
    low = lax.broadcasted_iota(jnp.int32, (1, LANES), 1) < COLS
    for values, f in ((keep, core), (received, 1 - core)):
        out[f, 0] = jnp.where(low, values[0], pltpu.roll(values[1], COLS, 1))
        out[f, 1] = jnp.where(low, pltpu.roll(values[0], COLS, 1), values[1])


def finish(keep, received):
    return pl.pallas_call(
        finish_kernel,
        out_shape=jax.ShapeDtypeStruct((2, 2, ROWS, LANES), jnp.float32),
        in_specs=[vmem()] * 2,
        out_specs=vmem(),
        compiler_params=params(),
        cost_estimate=pl.CostEstimate(flops=1_000_000, bytes_accessed=1_000_000, transcendentals=0),
        name="finish",
    )(keep, received)


def shards(source_spectrum, surf_freq, centers, counts):
    surf_t = jnp.swapaxes(surf_freq, 2, 3)
    inputs = (source_spectrum, surf_t, counts.reshape(HALF // LANES, LANES), centers)
    received = lax.ppermute(prepare(True, *inputs), AXES, CORE_PAIRS)
    kept = prepare(False, *inputs)
    own, code = pack(kept, received)
    partner = lax.ppermute(own, AXES, HALF_PAIRS)
    gathered = lax.all_gather(code, AXES, axis_index_groups=ALONG_Z, axis=0)
    arrived = lax.all_to_all(product(own, partner, gathered), AXES, 0, 0, axis_index_groups=PLANE_CHIPS)
    keep, sent = add(arrived)
    return finish(keep, lax.ppermute(sent, AXES, CORE_PAIRS))


def solution(mesh):
    in_specs = (P(None, None, "src", "surf"), P(None, None, "surf", "src"), P("src"), P("surf"))
    out_specs = P(None, None, "src", "surf")
    return jax.shard_map(shards, mesh=mesh, in_specs=in_specs, out_specs=out_specs, check_vma=False)
```

```python
import functools
import itertools

import jax
import jax.numpy as jnp
from jax import lax
from jax.experimental import pallas as pl
from jax.experimental.pallas import tpu as pltpu
from jax.sharding import PartitionSpec as P

BLOCK = 32
APER = 2048
RAMP = 1024
AXES = ("surf", "src")
NX, NYL, NC, NZ, NH = 4, 2, 2, 16, 2
ROWS = 256
HALF = 512
LANES = 128
COLS = 64
MSG = 528
SHIFT = 31
VMEM_LIMIT = 24 * 1024 * 1024
ALL_VMEM = 62 * 1024 * 1024 + 512 * 1024


def flat(x, yl, c, z, h):
    return ((x * NYL + yl) * NC + c) * NZ * NH + z * NH + h


COORDS = list(itertools.product(range(NX), range(NYL), range(NC), range(NZ), range(NH)))


def groups(key):
    found = {}
    for place in COORDS:
        found.setdefault(key(*place), []).append(flat(*place))
    return list(found.values())


CORE_PAIRS = [(flat(*p), flat(p[0], p[1], 1 - p[2], p[3], p[4])) for p in COORDS]
HALF_PAIRS = [(flat(*p), flat(p[0], p[1], p[2], p[3], 1 - p[4])) for p in COORDS]
ALONG_Z = groups(lambda x, yl, c, z, h: (x, yl, c, h))
PLANE_CHIPS = groups(lambda x, yl, c, z, h: (c, z))


def params(limit=VMEM_LIMIT):
    return pltpu.CompilerParams(vmem_limit_bytes=limit)


def vmem():
    return pl.BlockSpec(memory_space=pltpu.VMEM)


def anywhere():
    return pl.BlockSpec(memory_space=pl.ANY)


def core_index():
    return lax.rem(lax.axis_index("surf"), NC)


def half_index():
    return lax.rem(lax.axis_index("src"), NH)


def prepare_kernel(to_send, spectrum_in, surf_in, counts_in, centers_in, out, spectrum, surf, counts, centers, sems):
    f = 1 - core_index() if to_send else core_index()
    copies = [
        pltpu.make_async_copy(counts_in, counts, sems.at[0]),
        pltpu.make_async_copy(centers_in, centers, sems.at[1]),
        pltpu.make_async_copy(surf_in.at[f], surf, sems.at[2]),
        pltpu.make_async_copy(spectrum_in.at[f], spectrum, sems.at[3]),
    ]
    for copy in copies:
        copy.start()
    for copy in copies[:3]:
        copy.wait()
    column = lax.axis_index("src") * COLS + lax.broadcasted_iota(jnp.int32, (COLS, LANES), 0)
    for piece in range(HALF // LANES):
        lanes = slice(piece * LANES, (piece + 1) * LANES)
        live = column < counts[piece : piece + 1, :]
        for part in range(2):
            values = jnp.where(live, surf[part, :, lanes].astype(jnp.float32), 0.0).astype(jnp.bfloat16)
            out[2 * ROWS + part * COLS : 2 * ROWS + (part + 1) * COLS, lanes] = values
    copies[3].wait()
    first = lax.axis_index("surf") * HALF
    positions = (first + lax.broadcasted_iota(jnp.int32, (1, HALF), 1)).astype(jnp.float32)
    for block in range(ROWS // BLOCK):
        rows = slice(block * BLOCK, (block + 1) * BLOCK)
        distance = jnp.abs(positions - centers[block].astype(jnp.float32))
        taper = jnp.clip((APER + RAMP - distance) / RAMP, 0.0, 1.0)
        for part in range(2):
            values = (spectrum[part, rows, :].astype(jnp.float32) * taper).astype(jnp.bfloat16)
            out[part * ROWS + block * BLOCK : part * ROWS + (block + 1) * BLOCK, :] = values


def prepare(to_send, spectrum, surf, counts, centers):
    return pl.pallas_call(
        functools.partial(prepare_kernel, to_send),
        out_shape=jax.ShapeDtypeStruct((2 * ROWS + 2 * COLS, HALF), jnp.bfloat16),
        in_specs=[anywhere()] * 4,
        out_specs=vmem(),
        scratch_shapes=[
            pltpu.VMEM((2, ROWS, HALF), jnp.bfloat16),
            pltpu.VMEM((2, COLS, HALF), jnp.bfloat16),
            pltpu.VMEM((HALF // LANES, LANES), jnp.int32),
            pltpu.SMEM((ROWS // BLOCK,), jnp.int32),
            pltpu.SemaphoreType.DMA((4,)),
        ],
        compiler_params=params(ALL_VMEM if to_send else VMEM_LIMIT),
        cost_estimate=pl.CostEstimate(flops=2_000_000_000, bytes_accessed=3_000_000, transcendentals=0),
        name="prepare_sent" if to_send else "prepare_kept",
    )(spectrum, surf, counts, centers)


def encode(values):
    values = values.astype(jnp.float32)
    size = jnp.abs(values)
    exponent = jnp.floor(jnp.log2(jnp.maximum(size, 2.0**-126)) + 0.002)
    mantissa = jnp.round((size * 2.0**64) * jnp.exp2(-57.0 - exponent))
    down = jnp.clip(-4.0 - exponent, 0.0, 127.0)
    code = jnp.where(values < 0, -mantissa, mantissa) * 128.0 + down
    return jnp.where(size == 0, 0.0, code).astype(jnp.int32).astype(jnp.int16)


def pack_kernel(kept, received, a, code):
    core = core_index()
    for values, which in ((kept, core), (received, 1 - core)):
        place = pl.multiple_of(which * HALF, HALF)
        code[:, pl.ds(place, HALF)] = encode(values[2 * ROWS :, :])
        for part in range(2):
            columns = pl.ds(pl.multiple_of(part * 2 * HALF + place, HALF), HALF)
            a[:, columns] = values[part * ROWS : (part + 1) * ROWS, :]


def pack(kept, received):
    return pl.pallas_call(
        pack_kernel,
        out_shape=[
            jax.ShapeDtypeStruct((ROWS, 4 * HALF), jnp.bfloat16),
            jax.ShapeDtypeStruct((2 * COLS, 2 * HALF), jnp.int16),
        ],
        in_specs=[vmem()] * 2,
        out_specs=[vmem()] * 2,
        compiler_params=params(),
        cost_estimate=pl.CostEstimate(flops=2_000_000, bytes_accessed=2_500_000, transcendentals=300_000),
        name="pack",
    )(kept, received)


def exponent_of(largest):
    return jnp.floor(jnp.log2(jnp.maximum(largest, 2.0**-100)) + 0.002) + 1.0


def store_scaled(out, tiles, shift):
    exponents = []
    for which, values in enumerate(tiles):
        exponent = exponent_of(jnp.max(jnp.abs(values), axis=0, keepdims=True))
        scaled = jnp.clip(jnp.round(values * jnp.exp2(15.0 - exponent)), -32767.0, 32767.0)
        out[which * ROWS : (which + 1) * ROWS, :] = scaled.astype(jnp.int32).astype(jnp.int16)
        exponents.append(exponent - shift)
    row = lax.broadcasted_iota(jnp.int32, (MSG - 2 * ROWS, LANES), 0)
    out[2 * ROWS :, :] = jnp.where(row == 0, exponents[0], exponents[1]).astype(jnp.int32).astype(jnp.int16)


def load_scaled(message, which):
    below = message[2 * ROWS :, :].astype(jnp.int32).astype(jnp.float32)
    exponent = jnp.where(which == 0, below[0:1, :], below[1:2, :])
    values = message[pl.ds(pl.multiple_of(which * ROWS, ROWS), ROWS), :]
    return values.astype(jnp.int32).astype(jnp.float32) * jnp.exp2(exponent - 15.0)


def decode_pair(gathered, pair, b):
    k = 2 * HALF
    for block in range(2):
        for part in range(2):
            code = gathered[2 * pair + block, part * COLS : (part + 1) * COLS, :].astype(jnp.int32)
            mantissa = lax.shift_right_arithmetic(code, 7).astype(jnp.float32)
            down = jnp.bitwise_and(code, 127).astype(jnp.float32)
            piece = (mantissa * jnp.exp2((SHIFT - 11.0) - down)).astype(jnp.bfloat16)
            straight = block * LANES + part * COLS
            crossed = block * LANES + (1 - part) * COLS
            b[straight : straight + COLS, :k] = piece
            b[crossed : crossed + COLS, k:] = piece if part == 0 else -piece


def product_kernel(own, partner, gathered, out, a, b_even, b_odd):
    half = half_index()
    a[pl.ds(pl.multiple_of(half * ROWS, ROWS), ROWS), :] = own[...]
    a[pl.ds(pl.multiple_of((1 - half) * ROWS, ROWS), ROWS), :] = partner[...]
    pairs = NZ // 2
    decode_pair(gathered, 0, b_even)
    for pair in range(pairs):
        now, later = (b_even, b_odd) if pair % 2 == 0 else (b_odd, b_even)
        if pair + 1 < pairs:
            decode_pair(gathered, pair + 1, later)
        values = lax.dot_general(a[...], now[...], (((1,), (1,)), ((), ())), preferred_element_type=jnp.float32)
        for half in range(2):
            rows = slice(half * ROWS, (half + 1) * ROWS)
            store_scaled(out.at[2 * pair + half], (values[rows, :LANES], values[rows, LANES:]), SHIFT)


def product(own, partner, gathered):
    k = 2 * HALF
    return pl.pallas_call(
        product_kernel,
        out_shape=jax.ShapeDtypeStruct((16, MSG, LANES), jnp.int16),
        in_specs=[vmem()] * 3,
        out_specs=vmem(),
        scratch_shapes=[
            pltpu.VMEM((2 * ROWS, 2 * k), jnp.bfloat16),
            pltpu.VMEM((2 * LANES, 2 * k), jnp.bfloat16),
            pltpu.VMEM((2 * LANES, 2 * k), jnp.bfloat16),
        ],
        compiler_params=params(),
        cost_estimate=pl.CostEstimate(flops=4_300_000_000, bytes_accessed=9_000_000, transcendentals=2_000_000),
        name="product",
    )(own, partner, gathered)


def add_kernel(to_send, arrived, out):
    which = 1 - core_index() if to_send else core_index()
    for half in range(2):
        total = load_scaled(arrived.at[half], which)
        for chip in range(1, 8):
            total = total + load_scaled(arrived.at[2 * chip + half], which)
        out[half] = total


def add(to_send, arrived):
    return pl.pallas_call(
        functools.partial(add_kernel, to_send),
        out_shape=jax.ShapeDtypeStruct((2, ROWS, LANES), jnp.float32),
        in_specs=[vmem()],
        out_specs=vmem(),
        compiler_params=params(),
        cost_estimate=pl.CostEstimate(flops=2_000_000, bytes_accessed=1_500_000, transcendentals=0),
        name="add_sent" if to_send else "add_kept",
    )(arrived)


def finish_kernel(keep, received, out):
    core = core_index()
    low = lax.broadcasted_iota(jnp.int32, (1, LANES), 1) < COLS
    for values, f in ((keep, core), (received, 1 - core)):
        out[f, 0] = jnp.where(low, values[0], pltpu.roll(values[1], COLS, 1))
        out[f, 1] = jnp.where(low, pltpu.roll(values[0], COLS, 1), values[1])


def finish(keep, received):
    return pl.pallas_call(
        finish_kernel,
        out_shape=jax.ShapeDtypeStruct((2, 2, ROWS, LANES), jnp.float32),
        in_specs=[vmem()] * 2,
        out_specs=vmem(),
        compiler_params=params(),
        cost_estimate=pl.CostEstimate(flops=1_000_000, bytes_accessed=1_000_000, transcendentals=0),
        name="finish",
    )(keep, received)


def shards(source_spectrum, surf_freq, centers, counts):
    surf_t = jnp.swapaxes(surf_freq, 2, 3)
    inputs = (source_spectrum, surf_t, counts.reshape(HALF // LANES, LANES), centers)
    received = lax.ppermute(prepare(True, *inputs), AXES, CORE_PAIRS)
    kept = prepare(False, *inputs)
    own, code = pack(kept, received)
    partner = lax.ppermute(own, AXES, HALF_PAIRS)
    gathered = lax.all_gather(code, AXES, axis_index_groups=ALONG_Z, axis=0)
    arrived = lax.all_to_all(product(own, partner, gathered), AXES, 0, 0, axis_index_groups=PLANE_CHIPS)
    received = lax.ppermute(add(True, arrived), AXES, CORE_PAIRS)
    return finish(add(False, arrived), received)


def solution(mesh):
    in_specs = (P(None, None, "src", "surf"), P(None, None, "surf", "src"), P("src"), P("surf"))
    out_specs = P(None, None, "src", "surf")
    return jax.shard_map(shards, mesh=mesh, in_specs=in_specs, out_specs=out_specs, check_vma=False)
```

```python
import functools
import itertools

import jax
import jax.numpy as jnp
from jax import lax
from jax.experimental import pallas as pl
from jax.experimental.pallas import tpu as pltpu
from jax.sharding import PartitionSpec as P

BLOCK = 32
APER = 2048
RAMP = 1024
AXES = ("surf", "src")
NX, NYL, NC, NZ, NH = 4, 2, 2, 16, 2
ROWS = 256
HALF = 512
LANES = 128
COLS = 64
MSG = 528
SHIFT = 31
VMEM_LIMIT = 24 * 1024 * 1024
ALL_VMEM = 62 * 1024 * 1024 + 512 * 1024


def flat(x, yl, c, z, h):
    return ((x * NYL + yl) * NC + c) * NZ * NH + z * NH + h


COORDS = list(itertools.product(range(NX), range(NYL), range(NC), range(NZ), range(NH)))


def groups(key):
    found = {}
    for place in COORDS:
        found.setdefault(key(*place), []).append(flat(*place))
    return list(found.values())


CORE_PAIRS = [(flat(*p), flat(p[0], p[1], 1 - p[2], p[3], p[4])) for p in COORDS]
HALF_PAIRS = [(flat(*p), flat(p[0], p[1], p[2], p[3], 1 - p[4])) for p in COORDS]
ALONG_Z = groups(lambda x, yl, c, z, h: (x, yl, c, h))
PLANE_CHIPS = groups(lambda x, yl, c, z, h: (c, z))


def params(limit=VMEM_LIMIT):
    return pltpu.CompilerParams(vmem_limit_bytes=limit)


def vmem():
    return pl.BlockSpec(memory_space=pltpu.VMEM)


def anywhere():
    return pl.BlockSpec(memory_space=pl.ANY)


def core_index():
    return lax.rem(lax.axis_index("surf"), NC)


def half_index():
    return lax.rem(lax.axis_index("src"), NH)


def prepare_kernel(to_send, spectrum_in, surf_in, counts_in, centers_in, out, spectrum, surf, counts, centers, done, sems):
    f = 1 - core_index() if to_send else core_index()
    copies = [
        pltpu.make_async_copy(counts_in, counts, sems.at[0]),
        pltpu.make_async_copy(centers_in, centers, sems.at[1]),
        pltpu.make_async_copy(surf_in.at[f], surf, sems.at[2]),
        pltpu.make_async_copy(spectrum_in.at[f, 0], spectrum.at[0], sems.at[3]),
        pltpu.make_async_copy(spectrum_in.at[f, 1], spectrum.at[1], sems.at[4]),
    ]
    for copy in copies:
        copy.start()
    for copy in copies[:3]:
        copy.wait()
    result = done if to_send else out
    leaving = []

    def leave(rows):
        if to_send:
            leaving.append(pltpu.make_async_copy(done.at[rows], out.at[rows], sems.at[5 + len(leaving)]))
            leaving[-1].start()

    column = lax.axis_index("src") * COLS + lax.broadcasted_iota(jnp.int32, (COLS, LANES), 0)
    for piece in range(HALF // LANES):
        lanes = slice(piece * LANES, (piece + 1) * LANES)
        live = column < counts[piece : piece + 1, :]
        for part in range(2):
            values = jnp.where(live, surf[part, :, lanes].astype(jnp.float32), 0.0).astype(jnp.bfloat16)
            result[2 * ROWS + part * COLS : 2 * ROWS + (part + 1) * COLS, lanes] = values
    leave(slice(2 * ROWS, 2 * ROWS + 2 * COLS))
    first = lax.axis_index("surf") * HALF
    positions = (first + lax.broadcasted_iota(jnp.int32, (1, HALF), 1)).astype(jnp.float32)
    for part in range(2):
        copies[3 + part].wait()
        for block in range(ROWS // BLOCK):
            rows = slice(block * BLOCK, (block + 1) * BLOCK)
            distance = jnp.abs(positions - centers[block].astype(jnp.float32))
            taper = jnp.clip((APER + RAMP - distance) / RAMP, 0.0, 1.0)
            values = (spectrum[part, rows, :].astype(jnp.float32) * taper).astype(jnp.bfloat16)
            result[part * ROWS + block * BLOCK : part * ROWS + (block + 1) * BLOCK, :] = values
        leave(slice(part * ROWS, (part + 1) * ROWS))
    for copy in leaving:
        copy.wait()


def prepare(to_send, spectrum, surf, counts, centers):
    return pl.pallas_call(
        functools.partial(prepare_kernel, to_send),
        out_shape=jax.ShapeDtypeStruct((2 * ROWS + 2 * COLS, HALF), jnp.bfloat16),
        in_specs=[anywhere()] * 4,
        out_specs=anywhere() if to_send else vmem(),
        scratch_shapes=[
            pltpu.VMEM((2, ROWS, HALF), jnp.bfloat16),
            pltpu.VMEM((2, COLS, HALF), jnp.bfloat16),
            pltpu.VMEM((HALF // LANES, LANES), jnp.int32),
            pltpu.SMEM((ROWS // BLOCK,), jnp.int32),
            pltpu.VMEM((2 * ROWS + 2 * COLS, HALF), jnp.bfloat16),
            pltpu.SemaphoreType.DMA((8,)),
        ],
        compiler_params=params(ALL_VMEM if to_send else VMEM_LIMIT),
        cost_estimate=pl.CostEstimate(flops=2_000_000_000, bytes_accessed=3_000_000, transcendentals=0),
        name="prepare_sent" if to_send else "prepare_kept",
    )(spectrum, surf, counts, centers)


def encode(values):
    values = values.astype(jnp.float32)
    size = jnp.abs(values)
    exponent = jnp.floor(jnp.log2(jnp.maximum(size, 2.0**-126)) + 0.002)
    mantissa = jnp.round((size * 2.0**64) * jnp.exp2(-57.0 - exponent))
    down = jnp.clip(-4.0 - exponent, 0.0, 127.0)
    code = jnp.where(values < 0, -mantissa, mantissa) * 128.0 + down
    return jnp.where(size == 0, 0.0, code).astype(jnp.int32).astype(jnp.int16)


def pack_kernel(kept, received, a, code):
    core = core_index()
    for values, which in ((kept, core), (received, 1 - core)):
        place = pl.multiple_of(which * HALF, HALF)
        code[:, pl.ds(place, HALF)] = encode(values[2 * ROWS :, :])
        for part in range(2):
            columns = pl.ds(pl.multiple_of(part * 2 * HALF + place, HALF), HALF)
            a[:, columns] = values[part * ROWS : (part + 1) * ROWS, :]


def pack(kept, received):
    return pl.pallas_call(
        pack_kernel,
        out_shape=[
            jax.ShapeDtypeStruct((ROWS, 4 * HALF), jnp.bfloat16),
            jax.ShapeDtypeStruct((2 * COLS, 2 * HALF), jnp.int16),
        ],
        in_specs=[vmem()] * 2,
        out_specs=[vmem()] * 2,
        compiler_params=params(),
        cost_estimate=pl.CostEstimate(flops=2_000_000, bytes_accessed=2_500_000, transcendentals=300_000),
        name="pack",
    )(kept, received)


def exponent_of(largest):
    return jnp.floor(jnp.log2(jnp.maximum(largest, 2.0**-100)) + 0.002) + 1.0


def store_scaled(out, tiles, shift):
    exponents = []
    for which, values in enumerate(tiles):
        exponent = exponent_of(jnp.max(jnp.abs(values), axis=0, keepdims=True))
        scaled = jnp.clip(jnp.round(values * jnp.exp2(15.0 - exponent)), -32767.0, 32767.0)
        out[which * ROWS : (which + 1) * ROWS, :] = scaled.astype(jnp.int32).astype(jnp.int16)
        exponents.append(exponent - shift)
    row = lax.broadcasted_iota(jnp.int32, (MSG - 2 * ROWS, LANES), 0)
    out[2 * ROWS :, :] = jnp.where(row == 0, exponents[0], exponents[1]).astype(jnp.int32).astype(jnp.int16)


def load_scaled(message, which):
    below = message[2 * ROWS :, :].astype(jnp.int32).astype(jnp.float32)
    exponent = jnp.where(which == 0, below[0:1, :], below[1:2, :])
    values = message[pl.ds(pl.multiple_of(which * ROWS, ROWS), ROWS), :]
    return values.astype(jnp.int32).astype(jnp.float32) * jnp.exp2(exponent - 15.0)


def decode_pair(gathered, pair, b):
    k = 2 * HALF
    for block in range(2):
        for part in range(2):
            code = gathered[2 * pair + block, part * COLS : (part + 1) * COLS, :].astype(jnp.int32)
            mantissa = lax.shift_right_arithmetic(code, 7).astype(jnp.float32)
            down = jnp.bitwise_and(code, 127).astype(jnp.float32)
            piece = (mantissa * jnp.exp2((SHIFT - 11.0) - down)).astype(jnp.bfloat16)
            straight = block * LANES + part * COLS
            crossed = block * LANES + (1 - part) * COLS
            b[straight : straight + COLS, :k] = piece
            b[crossed : crossed + COLS, k:] = piece if part == 0 else -piece


def product_kernel(own, partner, gathered, out, a, b_even, b_odd):
    half = half_index()
    a[pl.ds(pl.multiple_of(half * ROWS, ROWS), ROWS), :] = own[...]
    a[pl.ds(pl.multiple_of((1 - half) * ROWS, ROWS), ROWS), :] = partner[...]
    pairs = NZ // 2
    decode_pair(gathered, 0, b_even)
    for pair in range(pairs):
        now, later = (b_even, b_odd) if pair % 2 == 0 else (b_odd, b_even)
        if pair + 1 < pairs:
            decode_pair(gathered, pair + 1, later)
        values = lax.dot_general(a[...], now[...], (((1,), (1,)), ((), ())), preferred_element_type=jnp.float32)
        for half in range(2):
            rows = slice(half * ROWS, (half + 1) * ROWS)
            store_scaled(out.at[2 * pair + half], (values[rows, :LANES], values[rows, LANES:]), SHIFT)


def product(own, partner, gathered):
    k = 2 * HALF
    return pl.pallas_call(
        product_kernel,
        out_shape=jax.ShapeDtypeStruct((16, MSG, LANES), jnp.int16),
        in_specs=[vmem()] * 3,
        out_specs=vmem(),
        scratch_shapes=[
            pltpu.VMEM((2 * ROWS, 2 * k), jnp.bfloat16),
            pltpu.VMEM((2 * LANES, 2 * k), jnp.bfloat16),
            pltpu.VMEM((2 * LANES, 2 * k), jnp.bfloat16),
        ],
        compiler_params=params(),
        cost_estimate=pl.CostEstimate(flops=4_300_000_000, bytes_accessed=9_000_000, transcendentals=2_000_000),
        name="product",
    )(own, partner, gathered)


def add_kernel(to_send, arrived, out):
    which = 1 - core_index() if to_send else core_index()
    for half in range(2):
        total = load_scaled(arrived.at[half], which)
        for chip in range(1, 8):
            total = total + load_scaled(arrived.at[2 * chip + half], which)
        out[half] = total


def add(to_send, arrived):
    return pl.pallas_call(
        functools.partial(add_kernel, to_send),
        out_shape=jax.ShapeDtypeStruct((2, ROWS, LANES), jnp.float32),
        in_specs=[vmem()],
        out_specs=vmem(),
        compiler_params=params(),
        cost_estimate=pl.CostEstimate(flops=2_000_000, bytes_accessed=1_500_000, transcendentals=0),
        name="add_sent" if to_send else "add_kept",
    )(arrived)


def finish_kernel(keep, received, out):
    core = core_index()
    low = lax.broadcasted_iota(jnp.int32, (1, LANES), 1) < COLS
    for values, f in ((keep, core), (received, 1 - core)):
        out[f, 0] = jnp.where(low, values[0], pltpu.roll(values[1], COLS, 1))
        out[f, 1] = jnp.where(low, pltpu.roll(values[0], COLS, 1), values[1])


def finish(keep, received):
    return pl.pallas_call(
        finish_kernel,
        out_shape=jax.ShapeDtypeStruct((2, 2, ROWS, LANES), jnp.float32),
        in_specs=[vmem()] * 2,
        out_specs=vmem(),
        compiler_params=params(),
        cost_estimate=pl.CostEstimate(flops=1_000_000, bytes_accessed=1_000_000, transcendentals=0),
        name="finish",
    )(keep, received)


def shards(source_spectrum, surf_freq, centers, counts):
    surf_t = jnp.swapaxes(surf_freq, 2, 3)
    inputs = (source_spectrum, surf_t, counts.reshape(HALF // LANES, LANES), centers)
    received = lax.ppermute(prepare(True, *inputs), AXES, CORE_PAIRS)
    kept = prepare(False, *inputs)
    own, code = pack(kept, received)
    partner = lax.ppermute(own, AXES, HALF_PAIRS)
    gathered = lax.all_gather(code, AXES, axis_index_groups=ALONG_Z, axis=0)
    arrived = lax.all_to_all(product(own, partner, gathered), AXES, 0, 0, axis_index_groups=PLANE_CHIPS)
    received = lax.ppermute(add(True, arrived), AXES, CORE_PAIRS)
    return finish(add(False, arrived), received)


def solution(mesh):
    in_specs = (P(None, None, "src", "surf"), P(None, None, "surf", "src"), P("src"), P("surf"))
    out_specs = P(None, None, "src", "surf")
    return jax.shard_map(shards, mesh=mesh, in_specs=in_specs, out_specs=out_specs, check_vma=False)
```

```python
import functools
import itertools

import jax
import jax.numpy as jnp
from jax import lax
from jax.experimental import pallas as pl
from jax.experimental.pallas import tpu as pltpu
from jax.sharding import PartitionSpec as P

BLOCK = 32
APER = 2048
RAMP = 1024
AXES = ("surf", "src")
NX, NYL, NC, NZ, NH = 4, 2, 2, 16, 2
ROWS = 256
HALF = 512
LANES = 128
COLS = 64
MSG = 528
SHIFT = 31
VMEM_LIMIT = 24 * 1024 * 1024
ALL_VMEM = 62 * 1024 * 1024 + 512 * 1024


def flat(x, yl, c, z, h):
    return ((x * NYL + yl) * NC + c) * NZ * NH + z * NH + h


COORDS = list(itertools.product(range(NX), range(NYL), range(NC), range(NZ), range(NH)))


def groups(key):
    found = {}
    for place in COORDS:
        found.setdefault(key(*place), []).append(flat(*place))
    return list(found.values())


CORE_PAIRS = [(flat(*p), flat(p[0], p[1], 1 - p[2], p[3], p[4])) for p in COORDS]
HALF_PAIRS = [(flat(*p), flat(p[0], p[1], p[2], p[3], 1 - p[4])) for p in COORDS]
ALONG_Z = groups(lambda x, yl, c, z, h: (x, yl, c, h))
PLANE_CHIPS = groups(lambda x, yl, c, z, h: (c, z))


def params(limit=VMEM_LIMIT):
    return pltpu.CompilerParams(vmem_limit_bytes=limit)


def vmem():
    return pl.BlockSpec(memory_space=pltpu.VMEM)


def anywhere():
    return pl.BlockSpec(memory_space=pl.ANY)


def core_index():
    return lax.rem(lax.axis_index("surf"), NC)


def half_index():
    return lax.rem(lax.axis_index("src"), NH)


def prepare_kernel(to_send, spectrum_in, surf_in, counts_in, centers_in, out, spectrum, surf, counts, centers, done, sems):
    f = 1 - core_index() if to_send else core_index()
    copies = [
        pltpu.make_async_copy(counts_in, counts, sems.at[0]),
        pltpu.make_async_copy(centers_in, centers, sems.at[1]),
        pltpu.make_async_copy(surf_in.at[f], surf, sems.at[2]),
        pltpu.make_async_copy(spectrum_in.at[f, 0], spectrum.at[0], sems.at[3]),
        pltpu.make_async_copy(spectrum_in.at[f, 1], spectrum.at[1], sems.at[4]),
    ]
    for copy in copies:
        copy.start()
    for copy in copies[:3]:
        copy.wait()
    result = done if to_send else out
    leaving = []

    def leave(rows):
        if to_send:
            leaving.append(pltpu.make_async_copy(done.at[rows], out.at[rows], sems.at[5 + len(leaving)]))
            leaving[-1].start()

    column = lax.axis_index("src") * COLS + lax.broadcasted_iota(jnp.int32, (COLS, LANES), 0)
    for piece in range(HALF // LANES):
        lanes = slice(piece * LANES, (piece + 1) * LANES)
        live = column < counts[piece : piece + 1, :]
        for part in range(2):
            values = jnp.where(live, surf[part, :, lanes].astype(jnp.float32), 0.0).astype(jnp.bfloat16)
            result[2 * ROWS + part * COLS : 2 * ROWS + (part + 1) * COLS, lanes] = values
    leave(slice(2 * ROWS, 2 * ROWS + 2 * COLS))
    first = lax.axis_index("surf") * HALF
    positions = (first + lax.broadcasted_iota(jnp.int32, (1, HALF), 1)).astype(jnp.float32)
    for part in range(2):
        copies[3 + part].wait()
        for block in range(ROWS // BLOCK):
            rows = slice(block * BLOCK, (block + 1) * BLOCK)
            distance = jnp.abs(positions - centers[block].astype(jnp.float32))
            taper = jnp.clip((APER + RAMP - distance) / RAMP, 0.0, 1.0)
            values = (spectrum[part, rows, :].astype(jnp.float32) * taper).astype(jnp.bfloat16)
            result[part * ROWS + block * BLOCK : part * ROWS + (block + 1) * BLOCK, :] = values
        leave(slice(part * ROWS, (part + 1) * ROWS))
    for copy in leaving:
        copy.wait()


def prepare(to_send, spectrum, surf, counts, centers):
    return pl.pallas_call(
        functools.partial(prepare_kernel, to_send),
        out_shape=jax.ShapeDtypeStruct((2 * ROWS + 2 * COLS, HALF), jnp.bfloat16),
        in_specs=[anywhere()] * 4,
        out_specs=anywhere() if to_send else vmem(),
        scratch_shapes=[
            pltpu.VMEM((2, ROWS, HALF), jnp.bfloat16),
            pltpu.VMEM((2, COLS, HALF), jnp.bfloat16),
            pltpu.VMEM((HALF // LANES, LANES), jnp.int32),
            pltpu.SMEM((ROWS // BLOCK,), jnp.int32),
            pltpu.VMEM((2 * ROWS + 2 * COLS, HALF), jnp.bfloat16),
            pltpu.SemaphoreType.DMA((8,)),
        ],
        compiler_params=params(ALL_VMEM if to_send else VMEM_LIMIT),
        cost_estimate=pl.CostEstimate(flops=2_000_000_000, bytes_accessed=3_000_000, transcendentals=0),
        name="prepare_sent" if to_send else "prepare_kept",
    )(spectrum, surf, counts, centers)


def encode(values):
    values = values.astype(jnp.float32)
    size = jnp.abs(values)
    exponent = jnp.floor(jnp.log2(jnp.maximum(size, 2.0**-126)) + 0.002)
    mantissa = jnp.round((size * 2.0**64) * jnp.exp2(-57.0 - exponent))
    down = jnp.clip(-4.0 - exponent, 0.0, 127.0)
    code = jnp.where(values < 0, -mantissa, mantissa) * 128.0 + down
    return jnp.where(size == 0, 0.0, code).astype(jnp.int32).astype(jnp.int16)


def pack_kernel(kept, received, a, code):
    core = core_index()
    for values, which in ((kept, core), (received, 1 - core)):
        place = pl.multiple_of(which * HALF, HALF)
        code[:, pl.ds(place, HALF)] = encode(values[2 * ROWS :, :])
        for part in range(2):
            columns = pl.ds(pl.multiple_of(part * 2 * HALF + place, HALF), HALF)
            a[:, columns] = values[part * ROWS : (part + 1) * ROWS, :]


def pack(kept, received):
    return pl.pallas_call(
        pack_kernel,
        out_shape=[
            jax.ShapeDtypeStruct((ROWS, 4 * HALF), jnp.bfloat16),
            jax.ShapeDtypeStruct((2 * COLS, 2 * HALF), jnp.int16),
        ],
        in_specs=[vmem()] * 2,
        out_specs=[vmem()] * 2,
        compiler_params=params(),
        cost_estimate=pl.CostEstimate(flops=2_000_000, bytes_accessed=2_500_000, transcendentals=300_000),
        name="pack",
    )(kept, received)


def exponent_of(largest):
    return jnp.floor(jnp.log2(jnp.maximum(largest, 2.0**-100)) + 0.002) + 1.0


def store_scaled(out, tiles, shift):
    exponents = []
    for which, values in enumerate(tiles):
        exponent = exponent_of(jnp.max(jnp.abs(values), axis=0, keepdims=True))
        scaled = jnp.clip(jnp.round(values * jnp.exp2(15.0 - exponent)), -32767.0, 32767.0)
        out[which * ROWS : (which + 1) * ROWS, :] = scaled.astype(jnp.int32).astype(jnp.int16)
        exponents.append(exponent - shift)
    row = lax.broadcasted_iota(jnp.int32, (MSG - 2 * ROWS, LANES), 0)
    out[2 * ROWS :, :] = jnp.where(row == 0, exponents[0], exponents[1]).astype(jnp.int32).astype(jnp.int16)


def load_scaled(message, which):
    below = message[2 * ROWS :, :].astype(jnp.int32).astype(jnp.float32)
    exponent = jnp.where(which == 0, below[0:1, :], below[1:2, :])
    values = message[pl.ds(pl.multiple_of(which * ROWS, ROWS), ROWS), :]
    return values.astype(jnp.int32).astype(jnp.float32) * jnp.exp2(exponent - 15.0)


def decode_pair(gathered, pair, b):
    k = 2 * HALF
    for block in range(2):
        for part in range(2):
            code = gathered[2 * pair + block, part * COLS : (part + 1) * COLS, :].astype(jnp.int32)
            mantissa = lax.shift_right_arithmetic(code, 7).astype(jnp.float32)
            down = jnp.bitwise_and(code, 127).astype(jnp.float32)
            piece = (mantissa * jnp.exp2((SHIFT - 11.0) - down)).astype(jnp.bfloat16)
            straight = block * LANES + part * COLS
            crossed = block * LANES + (1 - part) * COLS
            b[straight : straight + COLS, :k] = piece
            b[crossed : crossed + COLS, k:] = piece if part == 0 else -piece


def product_kernel(own, partner, gathered, out, a, b_even, b_odd):
    half = half_index()
    a[pl.ds(pl.multiple_of(half * ROWS, ROWS), ROWS), :] = own[...]
    a[pl.ds(pl.multiple_of((1 - half) * ROWS, ROWS), ROWS), :] = partner[...]
    pairs = NZ // 2
    decode_pair(gathered, 0, b_even)
    for pair in range(pairs):
        now, later = (b_even, b_odd) if pair % 2 == 0 else (b_odd, b_even)
        if pair + 1 < pairs:
            decode_pair(gathered, pair + 1, later)
        values = lax.dot_general(a[...], now[...], (((1,), (1,)), ((), ())), preferred_element_type=jnp.float32)
        for half in range(2):
            rows = slice(half * ROWS, (half + 1) * ROWS)
            store_scaled(out.at[2 * pair + half], (values[rows, :LANES], values[rows, LANES:]), SHIFT)


def product(own, partner, gathered):
    k = 2 * HALF
    return pl.pallas_call(
        product_kernel,
        out_shape=jax.ShapeDtypeStruct((16, MSG, LANES), jnp.int16),
        in_specs=[vmem()] * 3,
        out_specs=vmem(),
        scratch_shapes=[
            pltpu.VMEM((2 * ROWS, 2 * k), jnp.bfloat16),
            pltpu.VMEM((2 * LANES, 2 * k), jnp.bfloat16),
            pltpu.VMEM((2 * LANES, 2 * k), jnp.bfloat16),
        ],
        compiler_params=params(),
        cost_estimate=pl.CostEstimate(flops=4_300_000_000, bytes_accessed=9_000_000, transcendentals=2_000_000),
        name="product",
    )(own, partner, gathered)


def add_kernel(to_send, arrived, out):
    which = 1 - core_index() if to_send else core_index()
    for half in range(2):
        total = load_scaled(arrived.at[half], which)
        for chip in range(1, 8):
            total = total + load_scaled(arrived.at[2 * chip + half], which)
        out[half] = total


def add(to_send, arrived):
    return pl.pallas_call(
        functools.partial(add_kernel, to_send),
        out_shape=jax.ShapeDtypeStruct((2, ROWS, LANES), jnp.float32),
        in_specs=[vmem()],
        out_specs=vmem(),
        compiler_params=params(),
        cost_estimate=pl.CostEstimate(flops=2_000_000, bytes_accessed=1_500_000, transcendentals=0),
        name="add_sent" if to_send else "add_kept",
    )(arrived)


def finish_kernel(keep, received, out, done, sems):
    core = core_index()
    low = lax.broadcasted_iota(jnp.int32, (1, LANES), 1) < COLS
    leaving = []
    for which, (values, f) in enumerate(((keep, core), (received, 1 - core))):
        for part in range(2):
            if part == 0:
                done[which, part] = jnp.where(low, values[0], pltpu.roll(values[1], COLS, 1))
            else:
                done[which, part] = jnp.where(low, pltpu.roll(values[0], COLS, 1), values[1])
            leaving.append(pltpu.make_async_copy(done.at[which, part], out.at[f, part], sems.at[2 * which + part]))
            leaving[-1].start()
    for copy in leaving:
        copy.wait()


def finish(keep, received):
    return pl.pallas_call(
        finish_kernel,
        out_shape=jax.ShapeDtypeStruct((2, 2, ROWS, LANES), jnp.float32),
        in_specs=[vmem()] * 2,
        out_specs=anywhere(),
        scratch_shapes=[pltpu.VMEM((2, 2, ROWS, LANES), jnp.float32), pltpu.SemaphoreType.DMA((4,))],
        compiler_params=params(),
        cost_estimate=pl.CostEstimate(flops=1_000_000, bytes_accessed=1_000_000, transcendentals=0),
        name="finish",
    )(keep, received)


def shards(source_spectrum, surf_freq, centers, counts):
    surf_t = jnp.swapaxes(surf_freq, 2, 3)
    inputs = (source_spectrum, surf_t, counts.reshape(HALF // LANES, LANES), centers)
    received = lax.ppermute(prepare(True, *inputs), AXES, CORE_PAIRS)
    kept = prepare(False, *inputs)
    own, code = pack(kept, received)
    partner = lax.ppermute(own, AXES, HALF_PAIRS)
    gathered = lax.all_gather(code, AXES, axis_index_groups=ALONG_Z, axis=0)
    arrived = lax.all_to_all(product(own, partner, gathered), AXES, 0, 0, axis_index_groups=PLANE_CHIPS)
    received = lax.ppermute(add(True, arrived), AXES, CORE_PAIRS)
    return finish(add(False, arrived), received)


def solution(mesh):
    in_specs = (P(None, None, "src", "surf"), P(None, None, "surf", "src"), P("src"), P("surf"))
    out_specs = P(None, None, "src", "surf")
    return jax.shard_map(shards, mesh=mesh, in_specs=in_specs, out_specs=out_specs, check_vma=False)
```
